32 devices in a mesh: dp: 8 (over z, x), ctx: 4 (over y, core).
Axes of the slice: x: 2, y: 2, z: 4, core: 2. Of those that a mesh axis runs over, the one named last changes fastest.
Arguments:
- tokens: bfloat16 [8, 512, 640], P('dp', 'ctx'), may hold values from -6 to 6
- cotangent: bfloat16 [8, 512, 640], P('dp', 'ctx'), may hold values from -6 to 6
- segments: int32 [8, 512], P('dp', 'ctx'), may hold values from 0 to 3, never falling along the last dimension, each value on 1 to 384 neighbouring positions
- gains: bfloat16 [3072], P(('dp', 'ctx')), may hold values from 0.5 to 1.5
- w_query: bfloat16 [640, 1024], P(None, ('dp', 'ctx')), may hold values from -0.25 to 0.25
- w_key: bfloat16 [640, 256], P(None, ('dp', 'ctx')), may hold values from -0.25 to 0.25
- w_value: bfloat16 [640, 256], P(None, ('dp', 'ctx')), may hold values from -0.25 to 0.25
- w_out: bfloat16 [1024, 640], P(('dp', 'ctx')), may hold values from -0.1875 to 0.1875
- w_gate: bfloat16 [640, 2048], P(None, ('dp', 'ctx')), may hold values from -0.25 to 0.25
- w_up: bfloat16 [640, 2048], P(None, ('dp', 'ctx')), may hold values from -0.25 to 0.25
- w_down: bfloat16 [2048, 640], P(('dp', 'ctx')), may hold values from -0.125 to 0.125
Outputs:
- mixed: bfloat16 [8, 512, 640], P('dp', 'ctx')
- tokens_grad: bfloat16 [8, 512, 640], P('dp', 'ctx')
- gains_grad: float32 [3072], P(('dp', 'ctx'))
- w_query_grad: float32 [640, 1024], P(None, ('dp', 'ctx'))
- w_key_grad: float32 [640, 256], P(None, ('dp', 'ctx'))
- w_value_grad: float32 [640, 256], P(None, ('dp', 'ctx'))
- w_out_grad: float32 [1024, 640], P(('dp', 'ctx'))
- w_gate_grad: float32 [640, 2048], P(None, ('dp', 'ctx'))
- w_up_grad: float32 [640, 2048], P(None, ('dp', 'ctx'))
- w_down_grad: float32 [2048, 640], P(('dp', 'ctx'))
The draws below stay inside these ranges and needn't reach their ends.
Inputs may be any that keep to these rules, and one draw needn't show every extreme that they name: `segments`: each sequence holds 4 documents numbered in order, each of 1 to 384 tokens, one of exactly 384.
All inputs are finite; a program needn't handle non-finite values.
Results may differ from the reference program's by a relative error of at most 0.015.
Values may be sent and summed in bfloat16 or wider, within the bound.
A program may use at most 128 MiB of HBM per device.

```python
import math
import jax
import jax.numpy as jnp
import numpy as np
from jax import lax

D = 640
H = 4
HD = 256
FF = 2048
DOCS = 4
SEQ = 512
SEQS = 8


def block_scale(stream_key, shape, split, smallest, high):
    def one(position, blocks):
        draws = jax.random.uniform(jax.random.fold_in(jax.random.fold_in(stream_key, 6), position), (blocks,), jnp.float32, smallest / len(split), high / len(split))
        return jnp.repeat(jnp.exp(draws), shape[position] // blocks).reshape((-1,) + (1,) * (len(shape) - position - 1))

    level = one(*split[0])
    for cut in split[1:]:
        level = level * one(*cut)
    return level


def profile(amount, total, most, skew):
    weights = [(1 << 20) // math.isqrt(grade ** skew) + 1 for grade in range(2, amount + 1)]
    surplus, holding = total - most - (amount - 1), [1] * (amount - 1)
    while surplus > 0:
        candidates = [i for i in range(amount - 1) if holding[i] < most]
        mass, budget = sum([weights[i] for i in candidates]), surplus
        for i in candidates:
            extra = min(most - holding[i], max(1, budget * weights[i] // mass), surplus)
            holding[i] = holding[i] + extra
            surplus = surplus - extra
    return np.array([most] + holding)


def ragged_sizes(key, count, total, reach, lean):
    if count == 2:
        one = jax.random.randint(key, (), max(1, total - reach), min(reach, total - 1) + 1)
        return jnp.stack([one, total - one])
    lengths = jnp.asarray(profile(count, total, reach, lean), jnp.int32)
    couples = (count - 1) // 2
    giver, receiver = lengths[1:1 + 2 * couples:2], lengths[2:2 + 2 * couples:2]
    room = jnp.minimum(giver - 1, reach - receiver)
    shifted = jax.random.randint(jax.random.fold_in(key, 1), (couples,), 0, 1 << 20) % (room + 1)
    lengths = lengths.at[1:1 + 2 * couples:2].set(giver - shifted).at[2:2 + 2 * couples:2].set(receiver + shifted)
    return lengths[jax.random.permutation(jax.random.fold_in(key, 2), count)]


def centred(key, shape, scale, most, shards=(), kind=jnp.bfloat16):
    entries = jax.random.normal(key, shape, jnp.float32) * scale
    if len(shards) > 0:
        entries = block_scale(key, shape, shards, -0.22, 0.18) * entries
    return jnp.clip(entries, min=-most, max=most).astype(kind)


def setup_inputs(seed: int = 0) -> dict:
    key_of = jax.random.split(jax.random.key(seed), 12)
    tokens = centred(key_of[0], (SEQS, SEQ, D), 1.0, 6.0, ((0, 8), (1, 4)))
    cotangent = centred(key_of[1], (SEQS, SEQ, D), 1.0, 6.0, ((0, 8), (1, 4)))
    segments = jax.vmap(lambda own: jnp.searchsorted(jnp.cumsum(ragged_sizes(own, DOCS, SEQ, 3 * SEQ // 4, 0)), jnp.arange(SEQ), side="right"))(jax.random.split(key_of[2], SEQS)).reshape((SEQS, SEQ)).astype(jnp.int32)
    gains = jnp.clip(0.5 + 1.0 * jax.random.uniform(key_of[3], (4 * D + 2 * HD,), jnp.float32) ** block_scale(key_of[3], (4 * D + 2 * HD,), ((0, 32),), -0.2, 0.2), 0.5, 1.5).astype(jnp.bfloat16)
    w_query = centred(key_of[4], (D, H * HD), D ** -0.5, 0.25, ((1, 32),))
    w_key = centred(key_of[5], (D, HD), D ** -0.5, 0.25, ((1, 32),))
    w_value = centred(key_of[6], (D, HD), D ** -0.5, 0.25, ((1, 32),))
    w_out = centred(key_of[7], (H * HD, D), (H * HD) ** -0.5, 0.1875, ((0, 32),))
    w_gate = centred(key_of[8], (D, FF), D ** -0.5, 0.25, ((1, 32),))
    w_up = centred(key_of[9], (D, FF), D ** -0.5, 0.25, ((1, 32),))
    w_down = centred(key_of[10], (FF, D), FF ** -0.5, 0.125, ((0, 32),))
    return dict(tokens=tokens, cotangent=cotangent, segments=segments, gains=gains, w_query=w_query, w_key=w_key, w_value=w_value, w_out=w_out, w_gate=w_gate, w_up=w_up, w_down=w_down)


EPS = 1e-06
ROPE_BASE = 1000000.0
NEGATIVE = -1e+30

def rounded(value):
    return lax.optimization_barrier(value.astype(jnp.bfloat16))

def norm_forward(value, gain):
    factor = lax.rsqrt(lax.optimization_barrier(jnp.mean(value * value, axis=-1, keepdims=True)) + EPS)
    return (value * factor * gain, factor)

def norm_backward(value, factor, gain, grad_out):
    scaled = grad_out * gain
    grad_in = factor * scaled - value * (factor * factor * factor) * lax.optimization_barrier(jnp.mean(scaled * value, axis=-1, keepdims=True))
    grad_gain = lax.optimization_barrier(jnp.sum((grad_out * value * factor).reshape(-1, value.shape[-1]), axis=0))
    return (grad_in, grad_gain)

def rotary_tables(positions, width):
    exponent = jnp.arange(0, width, 2, dtype=jnp.int32).astype(jnp.float32) / width
    freqs = jnp.power(jnp.float32(ROPE_BASE), -exponent)
    theta = positions.astype(jnp.float32)[:, None] * freqs[None, :]
    return (jnp.cos(theta), jnp.sin(theta))

def rotate(value, cosine, sine):
    half = value.shape[-1] // 2
    first = value[..., :half]
    second = value[..., half:]
    return jnp.concatenate([first * cosine - second * sine, second * cosine + first * sine], axis=-1)

def product(left, right):
    return jnp.dot(left, right, preferred_element_type=jnp.float32)

def inner_rows(left, right):
    return lax.dot_general(left, right, (((0,), (0,)), ((), ())), preferred_element_type=jnp.float32)

def against(left, right):
    return lax.dot_general(left, right, (((1,), (1,)), ((), ())), preferred_element_type=jnp.float32)

def gelu_mix(gate_in, up_in):
    return jax.nn.gelu(gate_in, approximate=True) * up_in

def einsum_high(form, left, right):
    return jnp.einsum(form, left, right, precision=lax.Precision.HIGHEST)

def seq_pass(weights, gain_all, tokens_row, cot_row, seg_row):
    w_query, w_key, w_value, w_out, w_gate, w_up, w_down = weights
    seq = tokens_row.shape[0]
    g_in = gain_all[0:D]
    g_post_attn = gain_all[D:2 * D]
    g_pre_ff = gain_all[2 * D:3 * D]
    g_post_ff = gain_all[3 * D:4 * D]
    g_query = gain_all[4 * D:4 * D + HD]
    g_key = gain_all[4 * D + HD:4 * D + 2 * HD]
    scale = HD ** (-0.5)
    resid = tokens_row.astype(jnp.float32)
    normed_f, in_factor = norm_forward(resid, g_in)
    normed = rounded(normed_f)
    queries = product(normed, w_query).reshape(seq, H, HD)
    keys = product(normed, w_key)
    values = rounded(product(normed, w_value))
    positions = jnp.arange(seq, dtype=jnp.int32)
    cosine, sine = rotary_tables(positions, HD)
    query_normed, query_factor = norm_forward(queries, g_query)
    key_normed, key_factor = norm_forward(keys, g_key)
    query_rot = rounded(rotate(query_normed, cosine[:, None, :], sine[:, None, :]) * scale)
    key_rot = rounded(rotate(key_normed, cosine, sine))
    allowed = (positions[None, :] <= positions[:, None]) & (seg_row[None, :] == seg_row[:, None])
    scores = einsum_high('shd,td->hst', query_rot.astype(jnp.float32), key_rot.astype(jnp.float32))
    masked = jnp.where(allowed[None], scores, NEGATIVE)
    top = lax.optimization_barrier(jnp.max(masked, axis=-1, keepdims=True))
    raw = jnp.where(allowed[None], jnp.exp(masked - top), 0.0)
    log_total = top + jnp.log(lax.optimization_barrier(jnp.sum(raw, axis=-1, keepdims=True)))
    probs = jnp.where(allowed[None], jnp.exp(masked - log_total), 0.0)
    attended = einsum_high('hst,td->shd', probs, values.astype(jnp.float32))
    heads = rounded(attended.reshape(seq, H * HD))
    branch = product(heads, w_out)
    attn_normed, branch_factor = norm_forward(branch, g_post_attn)
    hidden = resid + attn_normed
    ff_f, ff_factor = norm_forward(hidden, g_pre_ff)
    ff_in = rounded(ff_f)
    gate = product(ff_in, w_gate)
    up_proj = product(ff_in, w_up)
    mid = rounded(gelu_mix(gate, up_proj))
    down = product(mid, w_down)
    down_normed, down_factor = norm_forward(down, g_post_ff)
    mixed = (hidden + down_normed).astype(jnp.bfloat16)
    grad_out = cot_row.astype(jnp.float32)
    grad_down_f, grad_g_post_ff = norm_backward(down, down_factor, g_post_ff, grad_out)
    grad_down = rounded(grad_down_f)
    w_down_grad = inner_rows(mid, grad_down)
    grad_mid = against(grad_down, w_down)
    _, gelu_back = jax.vjp(gelu_mix, gate, up_proj)
    grad_gate_f, grad_up_f = gelu_back(grad_mid)
    grad_gate = rounded(grad_gate_f)
    grad_up = rounded(grad_up_f)
    w_gate_grad = inner_rows(ff_in, grad_gate)
    w_up_grad = inner_rows(ff_in, grad_up)
    grad_ff = against(grad_gate, w_gate) + against(grad_up, w_up)
    hidden_part, grad_g_pre_ff = norm_backward(hidden, ff_factor, g_pre_ff, grad_ff)
    grad_hidden = grad_out + hidden_part
    grad_branch_f, grad_g_post_attn = norm_backward(branch, branch_factor, g_post_attn, grad_hidden)
    grad_branch = rounded(grad_branch_f)
    w_out_grad = inner_rows(heads, grad_branch)
    grad_att = rounded(against(grad_branch, w_out).reshape(seq, H, HD))
    grad_att_f = grad_att.astype(jnp.float32)
    delta = lax.optimization_barrier(jnp.sum(grad_att_f * attended, axis=-1))
    grad_probs = einsum_high('shd,td->hst', grad_att_f, values.astype(jnp.float32))
    grad_scores = rounded(probs * (grad_probs - jnp.transpose(delta)[:, :, None]))
    probs_low = rounded(probs).astype(jnp.float32)
    grad_values = rounded(einsum_high('hst,shd->td', probs_low, grad_att_f))
    grad_qrot = einsum_high('hst,td->shd', grad_scores.astype(jnp.float32), key_rot.astype(jnp.float32))
    grad_krot = einsum_high('hst,shd->td', grad_scores.astype(jnp.float32), query_rot.astype(jnp.float32))
    grad_qn = rotate(grad_qrot * scale, cosine[:, None, :], -sine[:, None, :])
    grad_queries_f, grad_g_query = norm_backward(queries, query_factor, g_query, grad_qn)
    grad_queries = rounded(grad_queries_f.reshape(seq, H * HD))
    grad_kn = rotate(grad_krot, cosine, -sine)
    grad_keys_f, grad_g_key = norm_backward(keys, key_factor, g_key, grad_kn)
    grad_keys = rounded(grad_keys_f)
    w_query_grad = inner_rows(normed, grad_queries)
    w_key_grad = inner_rows(normed, grad_keys)
    w_value_grad = inner_rows(normed, grad_values)
    grad_normed = against(grad_queries, w_query) + against(grad_keys, w_key) + against(grad_values, w_value)
    input_part, grad_g_in = norm_backward(resid, in_factor, g_in, grad_normed)
    tokens_grad = (grad_hidden + input_part).astype(jnp.bfloat16)
    gains_grad = jnp.concatenate([grad_g_in, grad_g_post_attn, grad_g_pre_ff, grad_g_post_ff, grad_g_query, grad_g_key])
    grads = (gains_grad, w_query_grad, w_key_grad, w_value_grad, w_out_grad, w_gate_grad, w_up_grad, w_down_grad)
    return (mixed, tokens_grad, grads)

def reference(tokens, cotangent, segments, gains, w_query, w_key, w_value, w_out, w_gate, w_up, w_down):
    weights = (w_query, w_key, w_value, w_out, w_gate, w_up, w_down)
    gain_all = gains.astype(jnp.float32)
    start = (jnp.zeros(gains.shape, jnp.float32), jnp.zeros(w_query.shape, jnp.float32), jnp.zeros(w_key.shape, jnp.float32), jnp.zeros(w_value.shape, jnp.float32), jnp.zeros(w_out.shape, jnp.float32), jnp.zeros(w_gate.shape, jnp.float32), jnp.zeros(w_up.shape, jnp.float32), jnp.zeros(w_down.shape, jnp.float32))

    def step(totals, item):
        tokens_row, cot_row, seg_row = item
        mixed_row, grad_row, grads = seq_pass(weights, gain_all, tokens_row, cot_row, seg_row)
        totals = jax.tree.map(lambda acc, new: acc + new, totals, grads)
        return (totals, (mixed_row, grad_row))
    totals, (mixed, tokens_grad) = lax.scan(step, start, (tokens, cotangent, segments))
    return (mixed, tokens_grad, totals[0], totals[1], totals[2], totals[3], totals[4], totals[5], totals[6], totals[7])
```

```python
import functools

import jax
import jax.numpy as jnp
from jax import lax
from jax.experimental import pallas as pl
from jax.experimental.pallas import tpu as pltpu
from jax.sharding import PartitionSpec as P

D = 640
H = 4
HD = 256

EPS = 1e-06
ROPE_BASE = 1000000.0
NEGATIVE = -1e30
MESH = pl.DeviceIdType.MESH
BF = jnp.bfloat16
F32 = jnp.float32


def norm_forward(value, gain):
    factor = lax.rsqrt(jnp.mean(value * value, axis=-1, keepdims=True) + EPS)
    return (value * factor * gain, factor)


def norm_backward(value, factor, gain, grad_out):
    scaled = grad_out * gain
    grad_in = factor * scaled - value * (factor * factor * factor) * jnp.mean(
        scaled * value, axis=-1, keepdims=True
    )
    grad_gain = jnp.sum((grad_out * value * factor).reshape(-1, value.shape[-1]), axis=0)
    return (grad_in, grad_gain)


def rotary_tables(positions, width):
    exponent = jnp.arange(0, width, 2, dtype=jnp.int32).astype(F32) / width
    freqs = jnp.power(F32(ROPE_BASE), -exponent)
    theta = positions.astype(F32)[:, None] * freqs[None, :]
    return (jnp.cos(theta), jnp.sin(theta))


def rotate(value, cosine, sine):
    half = value.shape[-1] // 2
    first = value[..., :half]
    second = value[..., half:]
    return jnp.concatenate(
        [first * cosine - second * sine, second * cosine + first * sine], axis=-1
    )


def product(left, right):
    return jnp.dot(left, right, preferred_element_type=F32)


def inner_rows(left, right):
    return lax.dot_general(left, right, (((0,), (0,)), ((), ())), preferred_element_type=F32)


def against(left, right):
    return lax.dot_general(left, right, (((1,), (1,)), ((), ())), preferred_element_type=F32)


def gelu_mix(gate_in, up_in):
    return jax.nn.gelu(gate_in, approximate=True) * up_in


Z = 4
ORDER = (0, 1, 3, 2)


def coordinates():
    dp = lax.axis_index("dp")
    ctx = lax.axis_index("ctx")
    return dp // 2, dp % 2, ctx // 2, ctx % 2


def slot(z, x, y, c):
    return (z * 2 + x) * 4 + y * 2 + c


def device(z, x, y, c):
    return (z * 2 + x, y * 2 + c)


def flip(bit, by):
    return 1 - bit if by else bit


def greet(peers):
    barrier = pltpu.get_barrier_semaphore()
    for peer in peers:
        pl.semaphore_signal(barrier, inc=1, device_id=peer, device_id_type=MESH)
    pl.semaphore_wait(barrier, len(peers))


def gather_kernel(cut, w_ref, t_ref, out, tout, send, recv, tsend, trecv, local):
    z, x, y, c = coordinates()
    rows = w_ref.shape[0]
    part = (pl.ds(0, cut), pl.ds(cut, rows - cut))
    to_z = {k: device((z + k) % Z, x, y, c) for k in (1, 2, 3)}
    to_x, to_y, to_c = device(z, 1 - x, y, c), device(z, x, 1 - y, c), device(z, x, y, 1 - c)
    to_d = device(z, x, 1 - y, 1 - c)
    greet([to_z[1], to_z[2], to_z[3], to_x, to_y, to_c, to_d])
    started = []

    def block(k, a, b, core):
        return slot((z + Z - k) % Z, flip(x, a), flip(y, b), core)

    def copy(index, source, target, peer, sends=send, recvs=recv):
        return pltpu.make_async_remote_copy(
            src_ref=source,
            dst_ref=target,
            send_sem=sends.at[index],
            recv_sem=recvs.at[index],
            device_id=peer,
            device_id_type=MESH,
        )

    def push(index, k, a, b, p, peer):
        where = block(k, a, b, c)
        source = w_ref.at[part[p]] if (k, a, b) == (0, 0, 0) else out.at[where, part[p]]
        one = copy(index, source, out.at[where, part[p]], peer)
        one.start()
        started.append(one)

    def arrived(index, k, a, b, p, core):
        where = out.at[block(k, a, b, core), part[p]]
        copy(index, where, where, to_c).wait_recv()

    def z_at(k, p):
        return (k - 1) * 2 + p

    def one_at(k, p):
        return 6 + k * 2 + p

    def two_at(k, j, p):
        return 14 + (k * 2 + j) * 2 + p

    def core_at(k, a, b, p):
        return 30 + ((k * 2 + a) * 2 + b) * 2 + p

    def sibling(k, a, b, p):
        push(core_at(k, a, b, p), k, a, b, p, to_c)

    def have_line(k):
        for p in range(2):
            push(one_at(k, p), k, 0, 0, p, (to_x, to_y)[p])
            push(two_at(k, 0, p), k, 0, 0, p, (to_y, to_x)[p])
        for p in range(2):
            sibling(k, 0, 0, p)

    mine = lax.axis_index("ctx")
    for i, peer in enumerate((to_c, to_y, to_d)):
        one = copy(i, t_ref, tout.at[mine], peer, tsend, trecv)
        one.start()
        started.append(one)
    keep = (
        pltpu.make_async_copy(t_ref, tout.at[mine], local.at[0]),
        pltpu.make_async_copy(w_ref, out.at[block(0, 0, 0, c)], local.at[1]),
    )
    for one in keep:
        one.start()
    for k in (1, 3, 2):
        for p in range(2):
            where = block(0, 0, 0, c)
            one = copy(z_at(k, p), w_ref.at[part[p]], out.at[where, part[p]], to_z[k])
            one.start()
            started.append(one)
    have_line(0)

    def have_one(k):
        for p in range(2):
            a, b = (1, 0) if p == 0 else (0, 1)
            arrived(one_at(k, p), k, a, b, p, c)
            push(two_at(k, 1, p), k, a, b, p, (to_y, to_x)[p])
            sibling(k, a, b, p)

    def have_two(k, j):
        for p in range(2):
            a, b = (j, 1) if p == 0 else (1, j)
            arrived(two_at(k, j, p), k, a, b, p, c)
            sibling(k, a, b, p)

    for step, k in enumerate(ORDER):
        if k:
            for p in range(2):
                arrived(z_at(k, p), k, 0, 0, p, c)
            have_line(k)
            have_one(ORDER[step - 1])
    have_one(ORDER[-1])
    for k in ORDER:
        have_two(k, 0)
    for k in ORDER:
        have_two(k, 1)
    for k in range(Z):
        for a in range(2):
            for b in range(2):
                for p in range(2):
                    arrived(core_at(k, a, b, p), k, a, b, p, 1 - c)
    for i, other in enumerate((y * 2 + 1 - c, (1 - y) * 2 + c, (1 - y) * 2 + 1 - c)):
        copy(i, t_ref, tout.at[other], to_c, tsend, trecv).wait_recv()
    for one in keep:
        one.wait()
    for one in started:
        one.wait_send()


def gather_call(packed, extra, devices, cycle):
    cut = packed.shape[0] // 32 * 16
    return pl.pallas_call(
        functools.partial(gather_kernel, cut),
        out_shape=(
            jax.ShapeDtypeStruct((devices,) + packed.shape, BF),
            jax.ShapeDtypeStruct((cycle,) + extra.shape, BF),
        ),
        in_specs=[pl.BlockSpec(memory_space=pl.ANY)] * 2,
        out_specs=[pl.BlockSpec(memory_space=pl.ANY)] * 2,
        scratch_shapes=[
            pltpu.SemaphoreType.DMA((62,)),
            pltpu.SemaphoreType.DMA((62,)),
            pltpu.SemaphoreType.DMA((3,)),
            pltpu.SemaphoreType.DMA((3,)),
            pltpu.SemaphoreType.DMA((2,)),
        ],
        compiler_params=pltpu.CompilerParams(collective_id=0, has_side_effects=True),
        name="gather_weights",
    )(packed, extra)


def reduce_kernel(cut, g_ref, out, cbuf, abuf, bbuf, zbuf, send, recv):
    z, x, y, c = coordinates()
    rows = g_ref.shape[1]
    part = (pl.ds(0, cut), pl.ds(cut, rows - cut))
    to_z = {k: device((z + k) % Z, x, y, c) for k in (1, 2, 3)}
    to_x, to_y, to_c = device(z, 1 - x, y, c), device(z, x, 1 - y, c), device(z, x, y, 1 - c)
    greet([to_z[1], to_z[2], to_z[3], to_x, to_y, to_c])
    started = []

    def push(index, source, target, peer):
        one = pltpu.make_async_remote_copy(
            src_ref=source,
            dst_ref=target,
            send_sem=send.at[index],
            recv_sem=recv.at[index],
            device_id=peer,
            device_id_type=MESH,
        )
        one.start()
        started.append(one)

    def arrived(index, target):
        pltpu.make_async_remote_copy(
            src_ref=target,
            dst_ref=target,
            send_sem=send.at[index],
            recv_sem=recv.at[index],
            device_id=to_c,
            device_id_type=MESH,
        ).wait_recv()

    def place(k, a, b):
        return (k * 2 + a) * 2 + b

    def block(k, a, b, core):
        return slot((z + k) % Z, flip(x, a), flip(y, b), core)

    far = [(k, a, b) for a, b in ((1, 1), (0, 1), (1, 0), (0, 0)) for k in (2, 1, 3, 0)]
    for k, a, b in far:
        i = place(k, a, b)
        push(i, g_ref.at[block(k, a, b, 1 - c)], cbuf.at[i], to_c)
    for k, a, b in far:
        i = place(k, a, b)
        arrived(i, cbuf.at[i])
        cbuf[i] = cbuf[i] + g_ref[block(k, a, b, c)]
        if b:
            j = k * 2 + a
            push(16 + j * 2, cbuf.at[i, part[0]], abuf.at[j, part[0]], to_y)
        if a:
            j = k * 2 + b
            push(17 + j * 2, cbuf.at[i, part[1]], abuf.at[j, part[1]], to_x)
    for near in (1, 0):
        for k in (2, 1, 3, 0):
            for p in range(2):
                j = k * 2 + near
                i = place(k, near, 0) if p == 0 else place(k, 0, near)
                arrived(16 + j * 2 + p, abuf.at[j, part[p]])
                abuf[j, part[p]] = abuf[j, part[p]] + cbuf[i, part[p]]
                if near:
                    push(
                        32 + k * 2 + p,
                        abuf.at[j, part[p]],
                        bbuf.at[k, part[p]],
                        (to_x, to_y)[p],
                    )
    for k in (2, 1, 3, 0):
        for p in range(2):
            arrived(32 + k * 2 + p, bbuf.at[k, part[p]])
            bbuf[k, part[p]] = bbuf[k, part[p]] + abuf[k * 2, part[p]]
            if k:
                push(
                    40 + (k - 1) * 2 + p,
                    bbuf.at[k, part[p]],
                    zbuf.at[k - 1, part[p]],
                    to_z[k],
                )
    out[...] = bbuf[0].astype(F32)
    for k in (1, 3, 2):
        for p in range(2):
            arrived(40 + (k - 1) * 2 + p, zbuf.at[k - 1, part[p]])
            out[part[p]] = out[part[p]] + zbuf[k - 1, part[p]].astype(F32)
    for one in started:
        one.wait_send()


def reduce_call(terms):
    shape = terms.shape[1:]
    cut = shape[0] // 32 * 16
    return pl.pallas_call(
        functools.partial(reduce_kernel, cut),
        out_shape=jax.ShapeDtypeStruct(shape, F32),
        in_specs=[pl.BlockSpec(memory_space=pltpu.VMEM)],
        out_specs=pl.BlockSpec(memory_space=pltpu.VMEM),
        scratch_shapes=[
            pltpu.VMEM((16,) + shape, BF),
            pltpu.VMEM((8,) + shape, BF),
            pltpu.VMEM((4,) + shape, BF),
            pltpu.VMEM((3,) + shape, BF),
            pltpu.SemaphoreType.DMA((46,)),
            pltpu.SemaphoreType.DMA((46,)),
        ],
        compiler_params=pltpu.CompilerParams(
            collective_id=1, has_side_effects=True, vmem_limit_bytes=48 * 1024 * 1024
        ),
        name="reduce_gradients",
    )(terms)


def exchange_kernel(g_ref, out, buf, send, recv):
    z, x, y, c = coordinates()
    others = ((y, 1 - c), (1 - y, c), (1 - y, 1 - c))
    greet([device(z, x, *other) for other in others])
    started = []
    for i in (2, 1, 0):
        yy, cc = others[i]
        one = pltpu.make_async_remote_copy(
            src_ref=g_ref.at[yy * 2 + cc],
            dst_ref=buf.at[i],
            send_sem=send.at[i],
            recv_sem=recv.at[i],
            device_id=device(z, x, yy, cc),
            device_id_type=MESH,
        )
        one.start()
        started.append(one)
    out[...] = g_ref[y * 2 + c].astype(F32)
    for one, i in zip(started[::-1], range(3)):
        one.wait_recv()
        out[...] = out[...] + buf[i].astype(F32)
    for one in started:
        one.wait_send()


def exchange_call(terms):
    shape = terms.shape[1:]
    return pl.pallas_call(
        exchange_kernel,
        out_shape=jax.ShapeDtypeStruct(shape, F32),
        in_specs=[pl.BlockSpec(memory_space=pltpu.VMEM)],
        out_specs=pl.BlockSpec(memory_space=pltpu.VMEM),
        scratch_shapes=[
            pltpu.VMEM((3,) + shape, BF),
            pltpu.SemaphoreType.DMA((3,)),
            pltpu.SemaphoreType.DMA((3,)),
        ],
        compiler_params=pltpu.CompilerParams(
            collective_id=2, has_side_effects=True, vmem_limit_bytes=16 * 1024 * 1024
        ),
        name="exchange_keys",
    )(terms)


def body(
    kernels, tokens, cotangent, segments, gains, w_query, w_key, w_value, w_out, w_gate, w_up, w_down
):
    resid = tokens[0].astype(F32)
    rows = resid.shape[0]
    cycle = lax.axis_size("ctx")
    groups = lax.axis_size("dp")
    devices = cycle * groups
    place = lax.axis_index("ctx")
    scale = HD ** (-0.5)
    doc_local = segments[0]
    own = (w_query.T, w_key.T, w_value.T, w_out, w_gate.T, w_up.T, w_down)
    own += (jnp.pad(gains[None], ((0, 0), (0, D - gains.shape[0]))),)
    counts = [piece.shape[0] for piece in own]
    starts = [sum(counts[:i]) for i in range(len(counts))]
    height = -(-sum(counts) // 16) * 16 if kernels else sum(counts)
    packed = jnp.pad(jnp.concatenate(own, axis=0), ((0, height - sum(counts)), (0, 0)))
    if kernels:
        marks = jnp.pad(doc_local.astype(BF)[None], ((0, 15), (0, D - rows)))
        every, near = gather_call(
            packed, jnp.concatenate([tokens[0], marks], axis=0), devices, cycle
        )
        tokens_all = near[:, :rows].reshape(cycle * rows, D)
        doc_all = near[:, rows, :rows].reshape(cycle * rows).astype(jnp.int32)
    else:
        every = lax.all_gather(packed, ("dp", "ctx"), axis=0, tiled=False)
        tokens_all = lax.all_gather(tokens[0], "ctx", axis=0, tiled=True)
        doc_all = lax.all_gather(doc_local, "ctx", axis=0, tiled=True)
    wq, wk, wv, wo, wg, wu, wd = [
        every[:, s : s + n].reshape(devices * n, D) for s, n in zip(starts[:7], counts[:7])
    ]
    gain_all = every[:, starts[7], : gains.shape[0]].reshape(-1).astype(F32)
    g_in = gain_all[0:D]
    g_post_attn = gain_all[D : 2 * D]
    g_pre_ff = gain_all[2 * D : 3 * D]
    g_post_ff = gain_all[3 * D : 4 * D]
    g_query = gain_all[4 * D : 4 * D + HD]
    g_key = gain_all[4 * D + HD : 4 * D + 2 * HD]

    normed_f, in_factor = norm_forward(resid, g_in)
    normed = normed_f.astype(BF)
    normed_all = norm_forward(tokens_all.astype(F32), g_in)[0].astype(BF)
    queries = against(normed, wq).reshape(rows, H, HD)
    keys_all = against(normed_all, wk)
    values_all = against(normed_all, wv).astype(BF)
    positions = place * rows + jnp.arange(rows, dtype=jnp.int32)
    cos_all, sin_all = rotary_tables(jnp.arange(cycle * rows, dtype=jnp.int32), HD)
    cosine = lax.dynamic_slice_in_dim(cos_all, place * rows, rows, 0)
    sine = lax.dynamic_slice_in_dim(sin_all, place * rows, rows, 0)
    query_normed, query_factor = norm_forward(queries, g_query)
    key_normed, key_factor_all = norm_forward(keys_all, g_key)
    keys = lax.dynamic_slice_in_dim(keys_all, place * rows, rows, 0)
    key_factor = lax.dynamic_slice_in_dim(key_factor_all, place * rows, rows, 0)
    query_rot = (rotate(query_normed, cosine[:, None, :], sine[:, None, :]) * scale).astype(BF)
    key_rot = rotate(key_normed, cos_all, sin_all).astype(BF)
    query_rows = jnp.transpose(query_rot, (1, 0, 2)).reshape(H * rows, HD)
    query_pos = jnp.tile(positions, H)
    query_doc = jnp.tile(doc_local, H)
    key_pos = jnp.arange(cycle * rows, dtype=jnp.int32)
    allowed = (key_pos[None, :] <= query_pos[:, None]) & (doc_all[None, :] == query_doc[:, None])
    masked = jnp.where(allowed, against(query_rows, key_rot), NEGATIVE)
    top = jnp.max(masked, axis=1, keepdims=True)
    weights = jnp.where(allowed, jnp.exp(masked - top), 0.0)
    probs = weights / jnp.sum(weights, axis=1, keepdims=True)
    probs_low = probs.astype(BF)
    probs_rest = (probs - probs_low.astype(F32)).astype(BF)
    attended_rows = product(probs_low, values_all) + product(probs_rest, values_all)
    attended = jnp.transpose(attended_rows.reshape(H, rows, HD), (1, 0, 2))
    heads = attended.reshape(rows, H * HD).astype(BF)
    branch = product(heads, wo)
    attn_normed, branch_factor = norm_forward(branch, g_post_attn)
    hidden = resid + attn_normed
    ff_f, ff_factor = norm_forward(hidden, g_pre_ff)
    ff_in = ff_f.astype(BF)
    gate = against(ff_in, wg)
    up_proj = against(ff_in, wu)
    mid = gelu_mix(gate, up_proj).astype(BF)
    down = product(mid, wd)
    down_normed, down_factor = norm_forward(down, g_post_ff)
    mixed = (hidden + down_normed).astype(BF)

    grad_out = cotangent[0].astype(F32)
    grad_down_f, grad_g_post_ff = norm_backward(down, down_factor, g_post_ff, grad_out)
    grad_down = grad_down_f.astype(BF)
    w_down_part = inner_rows(mid, grad_down)
    grad_mid = against(grad_down, wd)
    _, gelu_back = jax.vjp(gelu_mix, gate, up_proj)
    grad_gate_f, grad_up_f = gelu_back(grad_mid)
    grad_gate = grad_gate_f.astype(BF)
    grad_up = grad_up_f.astype(BF)
    w_gate_part = inner_rows(grad_gate, ff_in)
    w_up_part = inner_rows(grad_up, ff_in)
    grad_ff = product(grad_gate, wg) + product(grad_up, wu)
    hidden_part, grad_g_pre_ff = norm_backward(hidden, ff_factor, g_pre_ff, grad_ff)
    grad_hidden = grad_out + hidden_part
    grad_branch_f, grad_g_post_attn = norm_backward(branch, branch_factor, g_post_attn, grad_hidden)
    grad_branch = grad_branch_f.astype(BF)
    w_out_part = inner_rows(heads, grad_branch)
    grad_att = against(grad_branch, wo).reshape(rows, H, HD).astype(BF)
    grad_rows = jnp.transpose(grad_att, (1, 0, 2)).reshape(H * rows, HD)
    delta = jnp.sum(grad_rows.astype(F32) * attended_rows, axis=1, keepdims=True)
    grad_probs = against(grad_rows, values_all)
    grad_logits = (probs * (grad_probs - delta)).astype(BF)
    grad_qrows = product(grad_logits, key_rot)
    grad_key_part = inner_rows(grad_logits, query_rows)
    grad_value_part = inner_rows(probs_low, grad_rows)
    grad_kv = jnp.concatenate([grad_key_part, grad_value_part], axis=1)
    if kernels:
        key_grad = exchange_call(grad_kv.astype(BF).reshape(cycle, rows, 2 * HD))
    else:
        key_grad = lax.psum_scatter(grad_kv, "ctx", scatter_dimension=0, tiled=True)
    grad_krot = key_grad[:, :HD]
    grad_values = key_grad[:, HD:].astype(BF)
    grad_qrot = jnp.transpose(grad_qrows.reshape(H, rows, HD), (1, 0, 2))
    grad_qn = rotate(grad_qrot * scale, cosine[:, None, :], -sine[:, None, :])
    grad_queries_f, grad_g_query = norm_backward(queries, query_factor, g_query, grad_qn)
    grad_queries = grad_queries_f.reshape(rows, H * HD).astype(BF)
    grad_kn = rotate(grad_krot, cosine, -sine)
    grad_keys_f, grad_g_key = norm_backward(keys, key_factor, g_key, grad_kn)
    grad_keys = grad_keys_f.astype(BF)
    w_query_part = inner_rows(grad_queries, normed)
    w_key_part = inner_rows(grad_keys, normed)
    w_value_part = inner_rows(grad_values, normed)
    grad_normed = product(grad_queries, wq) + product(grad_keys, wk) + product(grad_values, wv)
    input_part, grad_g_in = norm_backward(resid, in_factor, g_in, grad_normed)
    tokens_grad = (grad_hidden + input_part).astype(BF)
    gains_part = jnp.concatenate(
        [grad_g_in, grad_g_post_attn, grad_g_pre_ff, grad_g_post_ff, grad_g_query, grad_g_key]
    ).reshape(devices, 1, -1)
    terms = [
        part.reshape(devices, -1, D)
        for part in (
            w_query_part,
            w_key_part,
            w_value_part,
            w_out_part,
            w_gate_part,
            w_up_part,
            w_down_part,
        )
    ]
    tail = ((0, 0), (0, height - sum(counts)), (0, D - gains.shape[0]))
    terms.append(jnp.pad(gains_part, tail))
    kind = BF if kernels else F32
    stacked = jnp.concatenate([term.astype(kind) for term in terms], axis=1)
    if kernels:
        owned = reduce_call(stacked)
    else:
        owned = lax.psum_scatter(stacked, ("dp", "ctx"), scatter_dimension=0, tiled=False)
    q, k, v, o, g, u, d, s = [owned[a : a + n] for a, n in zip(starts, counts)]
    return (
        mixed[None],
        tokens_grad[None],
        s[0, : gains.shape[0]],
        q.T,
        k.T,
        v.T,
        o,
        g.T,
        u.T,
        d,
    )


def solution(mesh):
    kernels = (mesh.shape["dp"], mesh.shape["ctx"]) == (8, 4)
    return jax.shard_map(
        functools.partial(body, kernels),
        mesh=mesh,
        in_specs=(
            P("dp", "ctx", None),
            P("dp", "ctx", None),
            P("dp", "ctx"),
            P(("dp", "ctx")),
            P(None, ("dp", "ctx")),
            P(None, ("dp", "ctx")),
            P(None, ("dp", "ctx")),
            P(("dp", "ctx"), None),
            P(None, ("dp", "ctx")),
            P(None, ("dp", "ctx")),
            P(("dp", "ctx"), None),
        ),
        out_specs=(
            P("dp", "ctx", None),
            P("dp", "ctx", None),
            P(("dp", "ctx")),
            P(None, ("dp", "ctx")),
            P(None, ("dp", "ctx")),
            P(None, ("dp", "ctx")),
            P(("dp", "ctx"), None),
            P(None, ("dp", "ctx")),
            P(None, ("dp", "ctx")),
            P(("dp", "ctx"), None),
        ),
        check_vma=False,
    )
```

```python
import functools

import jax
import jax.numpy as jnp
from jax import lax
from jax.experimental import pallas as pl
from jax.experimental.pallas import tpu as pltpu
from jax.sharding import PartitionSpec as P

D = 640
H = 4
HD = 256

EPS = 1e-06
ROPE_BASE = 1000000.0
NEGATIVE = -1e30
MESH = pl.DeviceIdType.MESH
BF = jnp.bfloat16
F32 = jnp.float32


def norm_forward(value, gain):
    factor = lax.rsqrt(jnp.mean(value * value, axis=-1, keepdims=True) + EPS)
    return (value * factor * gain, factor)


def norm_backward(value, factor, gain, grad_out):
    scaled = grad_out * gain
    grad_in = factor * scaled - value * (factor * factor * factor) * jnp.mean(
        scaled * value, axis=-1, keepdims=True
    )
    grad_gain = jnp.sum((grad_out * value * factor).reshape(-1, value.shape[-1]), axis=0)
    return (grad_in, grad_gain)


def rotary_tables(positions, width):
    exponent = jnp.arange(0, width, 2, dtype=jnp.int32).astype(F32) / width
    freqs = jnp.power(F32(ROPE_BASE), -exponent)
    theta = positions.astype(F32)[:, None] * freqs[None, :]
    return (jnp.cos(theta), jnp.sin(theta))


def rotate(value, cosine, sine):
    half = value.shape[-1] // 2
    first = value[..., :half]
    second = value[..., half:]
    return jnp.concatenate(
        [first * cosine - second * sine, second * cosine + first * sine], axis=-1
    )


def product(left, right):
    return jnp.dot(left, right, preferred_element_type=F32)


def inner_rows(left, right):
    return lax.dot_general(left, right, (((0,), (0,)), ((), ())), preferred_element_type=F32)


def against(left, right):
    return lax.dot_general(left, right, (((1,), (1,)), ((), ())), preferred_element_type=F32)


def gelu_mix(gate_in, up_in):
    return jax.nn.gelu(gate_in, approximate=True) * up_in


Z = 4
ORDER = (0, 1, 3, 2)


def coordinates():
    dp = lax.axis_index("dp")
    ctx = lax.axis_index("ctx")
    return dp // 2, dp % 2, ctx // 2, ctx % 2


def slot(z, x, y, c):
    return (z * 2 + x) * 4 + y * 2 + c


def device(z, x, y, c):
    return (z * 2 + x, y * 2 + c)


def flip(bit, by):
    return 1 - bit if by else bit


def greet(peers):
    barrier = pltpu.get_barrier_semaphore()
    for peer in peers:
        pl.semaphore_signal(barrier, inc=1, device_id=peer, device_id_type=MESH)
    pl.semaphore_wait(barrier, len(peers))


def gather_kernel(cut, w_ref, t_ref, out, tout, send, recv, tsend, trecv, local):
    z, x, y, c = coordinates()
    rows = w_ref.shape[0]
    part = (pl.ds(0, cut), pl.ds(cut, rows - cut))
    to_z = {k: device((z + k) % Z, x, y, c) for k in (1, 2, 3)}
    to_x, to_y, to_c = device(z, 1 - x, y, c), device(z, x, 1 - y, c), device(z, x, y, 1 - c)
    to_d = device(z, x, 1 - y, 1 - c)
    greet([to_z[1], to_z[2], to_z[3], to_x, to_y, to_c, to_d])
    started = []

    def block(k, a, b, core):
        return slot((z + Z - k) % Z, flip(x, a), flip(y, b), core)

    def copy(index, source, target, peer, sends=send, recvs=recv):
        return pltpu.make_async_remote_copy(
            src_ref=source,
            dst_ref=target,
            send_sem=sends.at[index],
            recv_sem=recvs.at[index],
            device_id=peer,
            device_id_type=MESH,
        )

    def push(index, k, a, b, p, peer):
        where = block(k, a, b, c)
        source = w_ref.at[part[p]] if (k, a, b) == (0, 0, 0) else out.at[where, part[p]]
        one = copy(index, source, out.at[where, part[p]], peer)
        one.start()
        started.append(one)

    def arrived(index, k, a, b, p, core):
        where = out.at[block(k, a, b, core), part[p]]
        copy(index, where, where, to_c).wait_recv()

    def z_at(k, p):
        return (k - 1) * 2 + p

    def one_at(k, p):
        return 6 + k * 2 + p

    def two_at(k, j, p):
        return 14 + (k * 2 + j) * 2 + p

    def core_at(k, a, b, p):
        return 30 + ((k * 2 + a) * 2 + b) * 2 + p

    def sibling(k, a, b, p):
        push(core_at(k, a, b, p), k, a, b, p, to_c)

    def have_line(k):
        for p in range(2):
            push(one_at(k, p), k, 0, 0, p, (to_x, to_y)[p])
            push(two_at(k, 0, p), k, 0, 0, p, (to_y, to_x)[p])
        for p in range(2):
            sibling(k, 0, 0, p)

    mine = lax.axis_index("ctx")
    for i, peer in enumerate((to_c, to_y, to_d)):
        one = copy(i, t_ref, tout.at[mine], peer, tsend, trecv)
        one.start()
        started.append(one)
    keep = (
        pltpu.make_async_copy(t_ref, tout.at[mine], local.at[0]),
        pltpu.make_async_copy(w_ref, out.at[block(0, 0, 0, c)], local.at[1]),
    )
    for one in keep:
        one.start()
    for k in (1, 3, 2):
        for p in range(2):
            where = block(0, 0, 0, c)
            one = copy(z_at(k, p), w_ref.at[part[p]], out.at[where, part[p]], to_z[k])
            one.start()
            started.append(one)
    have_line(0)

    def have_one(k):
        for p in range(2):
            a, b = (1, 0) if p == 0 else (0, 1)
            arrived(one_at(k, p), k, a, b, p, c)
            push(two_at(k, 1, p), k, a, b, p, (to_y, to_x)[p])
            sibling(k, a, b, p)

    def have_two(k, j):
        for p in range(2):
            a, b = (j, 1) if p == 0 else (1, j)
            arrived(two_at(k, j, p), k, a, b, p, c)
            sibling(k, a, b, p)

    for step, k in enumerate(ORDER):
        if k:
            for p in range(2):
                arrived(z_at(k, p), k, 0, 0, p, c)
            have_line(k)
            have_one(ORDER[step - 1])
    have_one(ORDER[-1])
    for k in ORDER:
        have_two(k, 0)
    for k in ORDER:
        have_two(k, 1)
    for k in range(Z):
        for a in range(2):
            for b in range(2):
                for p in range(2):
                    arrived(core_at(k, a, b, p), k, a, b, p, 1 - c)
    for i, other in enumerate((y * 2 + 1 - c, (1 - y) * 2 + c, (1 - y) * 2 + 1 - c)):
        copy(i, t_ref, tout.at[other], to_c, tsend, trecv).wait_recv()
    for one in keep:
        one.wait()
    for one in started:
        one.wait_send()


def takes(microseconds):
    return pl.CostEstimate(flops=0, transcendentals=0, bytes_accessed=microseconds * 3690000)


def gather_call(packed, extra, devices, cycle):
    cut = packed.shape[0] // 32 * 16
    return pl.pallas_call(
        functools.partial(gather_kernel, cut),
        out_shape=(
            jax.ShapeDtypeStruct((devices,) + packed.shape, BF),
            jax.ShapeDtypeStruct((cycle,) + extra.shape, BF),
        ),
        in_specs=[pl.BlockSpec(memory_space=pl.ANY)] * 2,
        out_specs=[pl.BlockSpec(memory_space=pl.ANY)] * 2,
        scratch_shapes=[
            pltpu.SemaphoreType.DMA((62,)),
            pltpu.SemaphoreType.DMA((62,)),
            pltpu.SemaphoreType.DMA((3,)),
            pltpu.SemaphoreType.DMA((3,)),
            pltpu.SemaphoreType.DMA((2,)),
        ],
        compiler_params=pltpu.CompilerParams(collective_id=0, has_side_effects=True),
        cost_estimate=takes(25),
        name="gather_weights",
    )(packed, extra)


def reduce_kernel(cut, g_ref, f_ref, out, fout, cbuf, abuf, bbuf, zbuf, fbuf, send, recv):
    z, x, y, c = coordinates()
    rows = g_ref.shape[1]
    part = (pl.ds(0, cut), pl.ds(cut, rows - cut))
    to_z = {k: device((z + k) % Z, x, y, c) for k in (1, 2, 3)}
    to_x, to_y, to_c = device(z, 1 - x, y, c), device(z, x, 1 - y, c), device(z, x, y, 1 - c)
    greet([to_z[1], to_z[2], to_z[3], to_x, to_y, to_c])
    started = []

    def push(index, source, target, peer):
        one = pltpu.make_async_remote_copy(
            src_ref=source,
            dst_ref=target,
            send_sem=send.at[index],
            recv_sem=recv.at[index],
            device_id=peer,
            device_id_type=MESH,
        )
        one.start()
        started.append(one)

    def arrived(index, target):
        pltpu.make_async_remote_copy(
            src_ref=target,
            dst_ref=target,
            send_sem=send.at[index],
            recv_sem=recv.at[index],
            device_id=to_c,
            device_id_type=MESH,
        ).wait_recv()

    def place(k, a, b):
        return (k * 2 + a) * 2 + b

    def block(k, a, b, core):
        return slot((z + k) % Z, flip(x, a), flip(y, b), core)

    far = [(k, a, b) for a, b in ((1, 1), (0, 1), (1, 0), (0, 0)) for k in (2, 1, 3, 0)]
    for k, a, b in far:
        i = place(k, a, b)
        push(i, g_ref.at[block(k, a, b, 1 - c)], cbuf.at[i], to_c)
    for k in (2, 1, 3):
        push(45 + k, f_ref.at[k], fbuf.at[k - 1], to_z[Z - k])
    for k, a, b in far:
        i = place(k, a, b)
        arrived(i, cbuf.at[i])
        cbuf[i] = cbuf[i] + g_ref[block(k, a, b, c)]
        if b:
            j = k * 2 + a
            push(16 + j * 2, cbuf.at[i, part[0]], abuf.at[j, part[0]], to_y)
        if a:
            j = k * 2 + b
            push(17 + j * 2, cbuf.at[i, part[1]], abuf.at[j, part[1]], to_x)
    for near in (1, 0):
        for k in (2, 1, 3, 0):
            for p in range(2):
                j = k * 2 + near
                i = place(k, near, 0) if p == 0 else place(k, 0, near)
                arrived(16 + j * 2 + p, abuf.at[j, part[p]])
                abuf[j, part[p]] = abuf[j, part[p]] + cbuf[i, part[p]]
                if near:
                    push(
                        32 + k * 2 + p,
                        abuf.at[j, part[p]],
                        bbuf.at[k, part[p]],
                        (to_x, to_y)[p],
                    )
    for k in (2, 1, 3, 0):
        for p in range(2):
            arrived(32 + k * 2 + p, bbuf.at[k, part[p]])
            bbuf[k, part[p]] = bbuf[k, part[p]] + abuf[k * 2, part[p]]
            if k:
                push(
                    40 + (k - 1) * 2 + p,
                    bbuf.at[k, part[p]],
                    zbuf.at[k - 1, part[p]],
                    to_z[k],
                )
    fout[...] = f_ref[0].astype(F32)
    for k in (1, 3, 2):
        arrived(45 + k, fbuf.at[k - 1])
        fout[...] = fout[...] + fbuf[k - 1].astype(F32)
    out[...] = bbuf[0].astype(F32)
    for k in (1, 3, 2):
        for p in range(2):
            arrived(40 + (k - 1) * 2 + p, zbuf.at[k - 1, part[p]])
            out[part[p]] = out[part[p]] + zbuf[k - 1, part[p]].astype(F32)
    for one in started:
        one.wait_send()


def reduce_call(terms, feed):
    shape = terms.shape[1:]
    cut = shape[0] // 32 * 16
    return pl.pallas_call(
        functools.partial(reduce_kernel, cut),
        out_shape=(
            jax.ShapeDtypeStruct(shape, F32),
            jax.ShapeDtypeStruct(feed.shape[1:], F32),
        ),
        in_specs=[pl.BlockSpec(memory_space=pltpu.VMEM)] * 2,
        out_specs=[pl.BlockSpec(memory_space=pltpu.VMEM)] * 2,
        scratch_shapes=[
            pltpu.VMEM((16,) + shape, BF),
            pltpu.VMEM((8,) + shape, BF),
            pltpu.VMEM((4,) + shape, BF),
            pltpu.VMEM((3,) + shape, BF),
            pltpu.VMEM((3,) + feed.shape[1:], BF),
            pltpu.SemaphoreType.DMA((49,)),
            pltpu.SemaphoreType.DMA((49,)),
        ],
        compiler_params=pltpu.CompilerParams(
            collective_id=1, has_side_effects=True, vmem_limit_bytes=32 * 1024 * 1024
        ),
        cost_estimate=takes(28),
        name="reduce_gradients",
    )(terms, feed)


def exchange_kernel(g_ref, out, buf, send, recv):
    z, x, y, c = coordinates()
    others = ((y, 1 - c), (1 - y, c), (1 - y, 1 - c))
    greet([device(z, x, *other) for other in others])
    started = []
    for i in (2, 1, 0):
        yy, cc = others[i]
        one = pltpu.make_async_remote_copy(
            src_ref=g_ref.at[yy * 2 + cc],
            dst_ref=buf.at[i],
            send_sem=send.at[i],
            recv_sem=recv.at[i],
            device_id=device(z, x, yy, cc),
            device_id_type=MESH,
        )
        one.start()
        started.append(one)
    out[...] = g_ref[y * 2 + c].astype(F32)
    for one, i in zip(started[::-1], range(3)):
        one.wait_recv()
        out[...] = out[...] + buf[i].astype(F32)
    for one in started:
        one.wait_send()


def exchange_call(terms):
    shape = terms.shape[1:]
    return pl.pallas_call(
        exchange_kernel,
        out_shape=jax.ShapeDtypeStruct(shape, F32),
        in_specs=[pl.BlockSpec(memory_space=pltpu.VMEM)],
        out_specs=pl.BlockSpec(memory_space=pltpu.VMEM),
        scratch_shapes=[
            pltpu.VMEM((3,) + shape, BF),
            pltpu.SemaphoreType.DMA((3,)),
            pltpu.SemaphoreType.DMA((3,)),
        ],
        compiler_params=pltpu.CompilerParams(
            collective_id=2, has_side_effects=True, vmem_limit_bytes=16 * 1024 * 1024
        ),
        cost_estimate=takes(9),
        name="exchange_keys",
    )(terms)


def move(value, axis, to):
    size = lax.axis_size(axis)
    return lax.ppermute(value, axis, [(i, to(i)) for i in range(size)])


def over_z(value, k):
    return move(value, "dp", lambda i: (i // 2 + k) % Z * 2 + i % 2)


def over_x(value):
    return move(value, "dp", lambda i: i ^ 1)


def over_y(value):
    return move(value, "ctx", lambda i: i ^ 2)


def over_core(value):
    return move(value, "ctx", lambda i: i ^ 1)


def halves(*pieces):
    return jnp.concatenate([p.reshape(2, p.shape[0] // 2, D) for p in pieces], axis=1)


def gather_feed(own):
    line = jnp.stack([own] + [over_z(own, k) for k in (1, 2, 3)])
    low, high = line[:, 0], line[:, 1]
    low = jnp.stack([low, over_x(low)])
    high = jnp.stack([high, over_y(high)])
    low = jnp.stack([low, over_y(low)])
    high = jnp.stack([high, over_x(high)])
    return jnp.stack([jnp.stack([low, high]), jnp.stack([over_core(low), over_core(high)])])


def reduce_over_core(terms):
    return [terms[0, p] + over_core(terms[1, p]) for p in range(2)]


def reduce_first(low, high):
    return [low[0] + over_y(low[1]), high[0] + over_x(high[1])]


def reduce_second(low, high):
    return [low[0] + over_x(low[1]), high[0] + over_y(high[1])]


def body(
    kernels, tokens, cotangent, segments, gains, w_query, w_key, w_value, w_out, w_gate, w_up, w_down
):
    resid = tokens[0].astype(F32)
    rows = resid.shape[0]
    cycle = lax.axis_size("ctx")
    groups = lax.axis_size("dp")
    devices = cycle * groups
    place = lax.axis_index("ctx")
    scale = HD ** (-0.5)
    doc_local = segments[0]
    own = (w_query.T, w_key.T, w_value.T, w_out)
    if kernels:
        feed = gather_feed(halves(w_gate.T, w_up.T, w_down))
    else:
        own += (w_gate.T, w_up.T, w_down)
    weights_held = len(own)
    own += (jnp.pad(gains[None], ((0, 0), (0, D - gains.shape[0]))),)
    counts = [piece.shape[0] for piece in own]
    starts = [sum(counts[:i]) for i in range(len(counts))]
    height = -(-sum(counts) // 16) * 16 if kernels else sum(counts)
    packed = jnp.pad(jnp.concatenate(own, axis=0), ((0, height - sum(counts)), (0, 0)))
    if kernels:
        marks = jnp.pad(doc_local.astype(BF)[None], ((0, 15), (0, D - rows)))
        every, near = gather_call(
            packed, jnp.concatenate([tokens[0], marks], axis=0), devices, cycle
        )
        tokens_all = near[:, :rows].reshape(cycle * rows, D)
        doc_all = near[:, rows, :rows].reshape(cycle * rows).astype(jnp.int32)
    else:
        every = lax.all_gather(packed, ("dp", "ctx"), axis=0, tiled=False)
        tokens_all = lax.all_gather(tokens[0], "ctx", axis=0, tiled=True)
        doc_all = lax.all_gather(doc_local, "ctx", axis=0, tiled=True)
    held = [
        every[:, s : s + n].reshape(devices * n, D)
        for s, n in zip(starts[:weights_held], counts[:weights_held])
    ]
    if kernels:
        third = feed.shape[-2] // 3
        held += [feed[..., i * third : (i + 1) * third, :].reshape(-1, D) for i in range(3)]
    wq, wk, wv, wo, wg, wu, wd = held
    gain_all = every[:, starts[weights_held], : gains.shape[0]].reshape(-1).astype(F32)
    g_in = gain_all[0:D]
    g_post_attn = gain_all[D : 2 * D]
    g_pre_ff = gain_all[2 * D : 3 * D]
    g_post_ff = gain_all[3 * D : 4 * D]
    g_query = gain_all[4 * D : 4 * D + HD]
    g_key = gain_all[4 * D + HD : 4 * D + 2 * HD]

    normed_f, in_factor = norm_forward(resid, g_in)
    normed = normed_f.astype(BF)
    normed_all = norm_forward(tokens_all.astype(F32), g_in)[0].astype(BF)
    queries = against(normed, wq).reshape(rows, H, HD)
    keys_all = against(normed_all, wk)
    values_all = against(normed_all, wv).astype(BF)
    positions = place * rows + jnp.arange(rows, dtype=jnp.int32)
    cos_all, sin_all = rotary_tables(jnp.arange(cycle * rows, dtype=jnp.int32), HD)
    cosine = lax.dynamic_slice_in_dim(cos_all, place * rows, rows, 0)
    sine = lax.dynamic_slice_in_dim(sin_all, place * rows, rows, 0)
    query_normed, query_factor = norm_forward(queries, g_query)
    key_normed, key_factor_all = norm_forward(keys_all, g_key)
    keys = lax.dynamic_slice_in_dim(keys_all, place * rows, rows, 0)
    key_factor = lax.dynamic_slice_in_dim(key_factor_all, place * rows, rows, 0)
    query_rot = (rotate(query_normed, cosine[:, None, :], sine[:, None, :]) * scale).astype(BF)
    key_rot = rotate(key_normed, cos_all, sin_all).astype(BF)
    query_rows = jnp.transpose(query_rot, (1, 0, 2)).reshape(H * rows, HD)
    query_pos = jnp.tile(positions, H)
    query_doc = jnp.tile(doc_local, H)
    key_pos = jnp.arange(cycle * rows, dtype=jnp.int32)
    allowed = (key_pos[None, :] <= query_pos[:, None]) & (doc_all[None, :] == query_doc[:, None])
    masked = jnp.where(allowed, against(query_rows, key_rot), NEGATIVE)
    top = jnp.max(masked, axis=1, keepdims=True)
    weights = jnp.where(allowed, jnp.exp(masked - top), 0.0)
    probs = weights / jnp.sum(weights, axis=1, keepdims=True)
    probs_low = probs.astype(BF)
    probs_rest = (probs - probs_low.astype(F32)).astype(BF)
    attended_rows = product(probs_low, values_all) + product(probs_rest, values_all)
    attended = jnp.transpose(attended_rows.reshape(H, rows, HD), (1, 0, 2))
    heads = attended.reshape(rows, H * HD).astype(BF)
    branch = product(heads, wo)
    attn_normed, branch_factor = norm_forward(branch, g_post_attn)
    hidden = resid + attn_normed
    ff_f, ff_factor = norm_forward(hidden, g_pre_ff)
    ff_in = ff_f.astype(BF)
    gate = against(ff_in, wg)
    up_proj = against(ff_in, wu)
    mid = gelu_mix(gate, up_proj).astype(BF)
    down = product(mid, wd)
    down_normed, down_factor = norm_forward(down, g_post_ff)
    mixed = (hidden + down_normed).astype(BF)

    grad_out = cotangent[0].astype(F32)
    grad_down_f, grad_g_post_ff = norm_backward(down, down_factor, g_post_ff, grad_out)
    grad_down = grad_down_f.astype(BF)
    w_down_part = inner_rows(mid, grad_down)
    grad_mid = against(grad_down, wd)
    _, gelu_back = jax.vjp(gelu_mix, gate, up_proj)
    grad_gate_f, grad_up_f = gelu_back(grad_mid)
    grad_gate = grad_gate_f.astype(BF)
    grad_up = grad_up_f.astype(BF)
    w_gate_part = inner_rows(grad_gate, ff_in)
    w_up_part = inner_rows(grad_up, ff_in)
    if kernels:
        feed_terms = [w_gate_part, w_up_part, w_down_part]
        shape = feed.shape[:-2] + (third, D)
        feed_sum = jnp.concatenate([term.astype(BF).reshape(shape) for term in feed_terms], axis=-2)
        feed_sum, grad_gate, grad_up = lax.optimization_barrier((feed_sum, grad_gate, grad_up))
        feed_sum = reduce_over_core(feed_sum)
    grad_ff = product(grad_gate, wg) + product(grad_up, wu)
    hidden_part, grad_g_pre_ff = norm_backward(hidden, ff_factor, g_pre_ff, grad_ff)
    grad_hidden = grad_out + hidden_part
    grad_branch_f, grad_g_post_attn = norm_backward(branch, branch_factor, g_post_attn, grad_hidden)
    grad_branch = grad_branch_f.astype(BF)
    w_out_part = inner_rows(heads, grad_branch)
    grad_att = against(grad_branch, wo).reshape(rows, H, HD).astype(BF)
    if kernels:
        feed_sum, grad_att = lax.optimization_barrier((feed_sum, grad_att))
        feed_sum = reduce_first(*feed_sum)
    grad_rows = jnp.transpose(grad_att, (1, 0, 2)).reshape(H * rows, HD)
    delta = jnp.sum(grad_rows.astype(F32) * attended_rows, axis=1, keepdims=True)
    grad_probs = against(grad_rows, values_all)
    grad_logits = (probs * (grad_probs - delta)).astype(BF)
    grad_qrows = product(grad_logits, key_rot)
    grad_key_part = inner_rows(grad_logits, query_rows)
    grad_value_part = inner_rows(probs_low, grad_rows)
    grad_kv = jnp.concatenate([grad_key_part, grad_value_part], axis=1)
    if kernels:
        key_grad = exchange_call(grad_kv.astype(BF).reshape(cycle, rows, 2 * HD))
        feed_sum, key_grad = lax.optimization_barrier((feed_sum, key_grad))
        feed_sum = reduce_second(*feed_sum)
    else:
        key_grad = lax.psum_scatter(grad_kv, "ctx", scatter_dimension=0, tiled=True)
    grad_krot = key_grad[:, :HD]
    grad_values = key_grad[:, HD:].astype(BF)
    grad_qrot = jnp.transpose(grad_qrows.reshape(H, rows, HD), (1, 0, 2))
    grad_qn = rotate(grad_qrot * scale, cosine[:, None, :], -sine[:, None, :])
    grad_queries_f, grad_g_query = norm_backward(queries, query_factor, g_query, grad_qn)
    grad_queries = grad_queries_f.reshape(rows, H * HD).astype(BF)
    grad_kn = rotate(grad_krot, cosine, -sine)
    grad_keys_f, grad_g_key = norm_backward(keys, key_factor, g_key, grad_kn)
    grad_keys = grad_keys_f.astype(BF)
    w_query_part = inner_rows(grad_queries, normed)
    w_key_part = inner_rows(grad_keys, normed)
    w_value_part = inner_rows(grad_values, normed)
    grad_normed = product(grad_queries, wq) + product(grad_keys, wk) + product(grad_values, wv)
    input_part, grad_g_in = norm_backward(resid, in_factor, g_in, grad_normed)
    tokens_grad = (grad_hidden + input_part).astype(BF)
    gains_part = jnp.concatenate(
        [grad_g_in, grad_g_post_attn, grad_g_pre_ff, grad_g_post_ff, grad_g_query, grad_g_key]
    ).reshape(devices, 1, -1)
    terms = [
        part.reshape(devices, -1, D)
        for part in (
            w_query_part,
            w_key_part,
            w_value_part,
            w_out_part,
            w_gate_part,
            w_up_part,
            w_down_part,
        )[:weights_held]
    ]
    tail = ((0, 0), (0, height - sum(counts)), (0, D - gains.shape[0]))
    terms.append(jnp.pad(gains_part, tail))
    kind = BF if kernels else F32
    stacked = jnp.concatenate([term.astype(kind) for term in terms], axis=1)
    if kernels:
        low, high = feed_sum
        owned, feed_owned = reduce_call(stacked, jnp.concatenate([low, high], axis=1))
        feed_owned = feed_owned.reshape(2, -1, D)
    else:
        owned = lax.psum_scatter(stacked, ("dp", "ctx"), scatter_dimension=0, tiled=False)
    parts = [owned[a : a + n] for a, n in zip(starts, counts)]
    s = parts.pop()
    if kernels:
        parts += [feed_owned[:, i * third : (i + 1) * third].reshape(-1, D) for i in range(3)]
    q, k, v, o, g, u, d = parts
    return (
        mixed[None],
        tokens_grad[None],
        s[0, : gains.shape[0]],
        q.T,
        k.T,
        v.T,
        o,
        g.T,
        u.T,
        d,
    )


def solution(mesh):
    kernels = (mesh.shape["dp"], mesh.shape["ctx"]) == (8, 4)
    return jax.shard_map(
        functools.partial(body, kernels),
        mesh=mesh,
        in_specs=(
            P("dp", "ctx", None),
            P("dp", "ctx", None),
            P("dp", "ctx"),
            P(("dp", "ctx")),
            P(None, ("dp", "ctx")),
            P(None, ("dp", "ctx")),
            P(None, ("dp", "ctx")),
            P(("dp", "ctx"), None),
            P(None, ("dp", "ctx")),
            P(None, ("dp", "ctx")),
            P(("dp", "ctx"), None),
        ),
        out_specs=(
            P("dp", "ctx", None),
            P("dp", "ctx", None),
            P(("dp", "ctx")),
            P(None, ("dp", "ctx")),
            P(None, ("dp", "ctx")),
            P(None, ("dp", "ctx")),
            P(("dp", "ctx"), None),
            P(None, ("dp", "ctx")),
            P(None, ("dp", "ctx")),
            P(("dp", "ctx"), None),
        ),
        check_vma=False,
    )
```

```python
import functools

import jax
import jax.numpy as jnp
from jax import lax
from jax.experimental import pallas as pl
from jax.experimental.pallas import tpu as pltpu
from jax.sharding import PartitionSpec as P

D = 640
H = 4
HD = 256

EPS = 1e-06
ROPE_BASE = 1000000.0
NEGATIVE = -1e30
MESH = pl.DeviceIdType.MESH
BF = jnp.bfloat16
F32 = jnp.float32


def norm_forward(value, gain):
    factor = lax.rsqrt(jnp.mean(value * value, axis=-1, keepdims=True) + EPS)
    return (value * factor * gain, factor)


def norm_backward(value, factor, gain, grad_out):
    scaled = grad_out * gain
    grad_in = factor * scaled - value * (factor * factor * factor) * jnp.mean(
        scaled * value, axis=-1, keepdims=True
    )
    grad_gain = jnp.sum((grad_out * value * factor).reshape(-1, value.shape[-1]), axis=0)
    return (grad_in, grad_gain)


def rotary_tables(positions, width):
    exponent = jnp.arange(0, width, 2, dtype=jnp.int32).astype(F32) / width
    freqs = jnp.power(F32(ROPE_BASE), -exponent)
    theta = positions.astype(F32)[:, None] * freqs[None, :]
    return (jnp.cos(theta), jnp.sin(theta))


def rotate(value, cosine, sine):
    half = value.shape[-1] // 2
    first = value[..., :half]
    second = value[..., half:]
    return jnp.concatenate(
        [first * cosine - second * sine, second * cosine + first * sine], axis=-1
    )


def product(left, right):
    return jnp.dot(left, right, preferred_element_type=F32)


def inner_rows(left, right):
    return lax.dot_general(left, right, (((0,), (0,)), ((), ())), preferred_element_type=F32)


def against(left, right):
    return lax.dot_general(left, right, (((1,), (1,)), ((), ())), preferred_element_type=F32)


def gelu_mix(gate_in, up_in):
    return jax.nn.gelu(gate_in, approximate=True) * up_in


Z = 4
ORDER = (0, 1, 3, 2)


def coordinates():
    dp = lax.axis_index("dp")
    ctx = lax.axis_index("ctx")
    return dp // 2, dp % 2, ctx // 2, ctx % 2


def slot(z, x, y, c):
    return (z * 2 + x) * 4 + y * 2 + c


def device(z, x, y, c):
    return (z * 2 + x, y * 2 + c)


def flip(bit, by):
    return 1 - bit if by else bit


def greet(peers):
    barrier = pltpu.get_barrier_semaphore()
    for peer in peers:
        pl.semaphore_signal(barrier, inc=1, device_id=peer, device_id_type=MESH)
    pl.semaphore_wait(barrier, len(peers))


def gather_kernel(cut, w_ref, t_ref, out, tout, send, recv, tsend, trecv, local):
    z, x, y, c = coordinates()
    rows = w_ref.shape[0]
    part = (pl.ds(0, cut), pl.ds(cut, rows - cut))
    to_z = {k: device((z + k) % Z, x, y, c) for k in (1, 2, 3)}
    to_x, to_y, to_c = device(z, 1 - x, y, c), device(z, x, 1 - y, c), device(z, x, y, 1 - c)
    to_d = device(z, x, 1 - y, 1 - c)
    greet([to_z[1], to_z[2], to_z[3], to_x, to_y, to_c, to_d])
    started = []

    def block(k, a, b, core):
        return slot((z + Z - k) % Z, flip(x, a), flip(y, b), core)

    def copy(index, source, target, peer, sends=send, recvs=recv):
        return pltpu.make_async_remote_copy(
            src_ref=source,
            dst_ref=target,
            send_sem=sends.at[index],
            recv_sem=recvs.at[index],
            device_id=peer,
            device_id_type=MESH,
        )

    def push(index, k, a, b, p, peer):
        where = block(k, a, b, c)
        source = w_ref.at[part[p]] if (k, a, b) == (0, 0, 0) else out.at[where, part[p]]
        one = copy(index, source, out.at[where, part[p]], peer)
        one.start()
        started.append(one)

    def arrived(index, k, a, b, p, core):
        where = out.at[block(k, a, b, core), part[p]]
        copy(index, where, where, to_c).wait_recv()

    def z_at(k, p):
        return (k - 1) * 2 + p

    def one_at(k, p):
        return 6 + k * 2 + p

    def two_at(k, j, p):
        return 14 + (k * 2 + j) * 2 + p

    def core_at(k, a, b, p):
        return 30 + ((k * 2 + a) * 2 + b) * 2 + p

    def sibling(k, a, b, p):
        push(core_at(k, a, b, p), k, a, b, p, to_c)

    def have_line(k):
        for p in range(2):
            push(one_at(k, p), k, 0, 0, p, (to_x, to_y)[p])
            push(two_at(k, 0, p), k, 0, 0, p, (to_y, to_x)[p])
        for p in range(2):
            sibling(k, 0, 0, p)

    mine = lax.axis_index("ctx")
    for i, peer in enumerate((to_c, to_y, to_d)):
        one = copy(i, t_ref, tout.at[mine], peer, tsend, trecv)
        one.start()
        started.append(one)
    keep = (
        pltpu.make_async_copy(t_ref, tout.at[mine], local.at[0]),
        pltpu.make_async_copy(w_ref, out.at[block(0, 0, 0, c)], local.at[1]),
    )
    for one in keep:
        one.start()
    for k in (1, 3, 2):
        for p in range(2):
            where = block(0, 0, 0, c)
            one = copy(z_at(k, p), w_ref.at[part[p]], out.at[where, part[p]], to_z[k])
            one.start()
            started.append(one)
    have_line(0)

    def have_one(k):
        for p in range(2):
            a, b = (1, 0) if p == 0 else (0, 1)
            arrived(one_at(k, p), k, a, b, p, c)
            push(two_at(k, 1, p), k, a, b, p, (to_y, to_x)[p])
            sibling(k, a, b, p)

    def have_two(k, j):
        for p in range(2):
            a, b = (j, 1) if p == 0 else (1, j)
            arrived(two_at(k, j, p), k, a, b, p, c)
            sibling(k, a, b, p)

    for step, k in enumerate(ORDER):
        if k:
            for p in range(2):
                arrived(z_at(k, p), k, 0, 0, p, c)
            have_line(k)
            have_one(ORDER[step - 1])
    have_one(ORDER[-1])
    for k in ORDER:
        have_two(k, 0)
    for k in ORDER:
        have_two(k, 1)
    for k in range(Z):
        for a in range(2):
            for b in range(2):
                for p in range(2):
                    arrived(core_at(k, a, b, p), k, a, b, p, 1 - c)
    for i, other in enumerate((y * 2 + 1 - c, (1 - y) * 2 + c, (1 - y) * 2 + 1 - c)):
        copy(i, t_ref, tout.at[other], to_c, tsend, trecv).wait_recv()
    for one in keep:
        one.wait()
    for one in started:
        one.wait_send()


def gather_call(packed, extra, devices, cycle):
    cut = packed.shape[0] // 32 * 16
    return pl.pallas_call(
        functools.partial(gather_kernel, cut),
        out_shape=(
            jax.ShapeDtypeStruct((devices,) + packed.shape, BF),
            jax.ShapeDtypeStruct((cycle,) + extra.shape, BF),
        ),
        in_specs=[pl.BlockSpec(memory_space=pl.ANY)] * 2,
        out_specs=[pl.BlockSpec(memory_space=pl.ANY)] * 2,
        scratch_shapes=[
            pltpu.SemaphoreType.DMA((62,)),
            pltpu.SemaphoreType.DMA((62,)),
            pltpu.SemaphoreType.DMA((3,)),
            pltpu.SemaphoreType.DMA((3,)),
            pltpu.SemaphoreType.DMA((2,)),
        ],
        compiler_params=pltpu.CompilerParams(collective_id=0, has_side_effects=True),
        name="gather_weights",
    )(packed, extra)


def reduce_kernel(cut, g_ref, out, lbuf, cbuf, abuf, bbuf, zbuf, send, recv, local):
    z, x, y, c = coordinates()
    rows = g_ref.shape[1]
    part = (pl.ds(0, cut), pl.ds(cut, rows - cut))
    to_z = {k: device((z + k) % Z, x, y, c) for k in (1, 2, 3)}
    to_x, to_y, to_c = device(z, 1 - x, y, c), device(z, x, 1 - y, c), device(z, x, y, 1 - c)
    greet([to_z[1], to_z[2], to_z[3], to_x, to_y, to_c])
    started = []

    def push(index, source, target, peer):
        one = pltpu.make_async_remote_copy(
            src_ref=source,
            dst_ref=target,
            send_sem=send.at[index],
            recv_sem=recv.at[index],
            device_id=peer,
            device_id_type=MESH,
        )
        one.start()
        started.append(one)

    def arrived(index, target):
        pltpu.make_async_remote_copy(
            src_ref=target,
            dst_ref=target,
            send_sem=send.at[index],
            recv_sem=recv.at[index],
            device_id=to_c,
            device_id_type=MESH,
        ).wait_recv()

    def place(k, a, b):
        return (k * 2 + a) * 2 + b

    def block(k, a, b, core):
        return slot((z + k) % Z, flip(x, a), flip(y, b), core)

    far = [(k, a, b) for a, b in ((1, 1), (0, 1), (1, 0), (0, 0)) for k in (2, 1, 3, 0)]
    for k, a, b in far:
        i = place(k, a, b)
        push(i, g_ref.at[block(k, a, b, 1 - c)], cbuf.at[i], to_c)
    held = {}
    for k, a, b in far:
        i = place(k, a, b)
        held[i] = pltpu.make_async_copy(g_ref.at[block(k, a, b, c)], lbuf.at[i], local.at[i])
        held[i].start()
    for k, a, b in far:
        i = place(k, a, b)
        arrived(i, cbuf.at[i])
        held[i].wait()
        cbuf[i] = cbuf[i] + lbuf[i]
        if b:
            j = k * 2 + a
            push(16 + j * 2, cbuf.at[i, part[0]], abuf.at[j, part[0]], to_y)
        if a:
            j = k * 2 + b
            push(17 + j * 2, cbuf.at[i, part[1]], abuf.at[j, part[1]], to_x)
    for near in (1, 0):
        for k in (2, 1, 3, 0):
            for p in range(2):
                j = k * 2 + near
                i = place(k, near, 0) if p == 0 else place(k, 0, near)
                arrived(16 + j * 2 + p, abuf.at[j, part[p]])
                abuf[j, part[p]] = abuf[j, part[p]] + cbuf[i, part[p]]
                if near:
                    push(
                        32 + k * 2 + p,
                        abuf.at[j, part[p]],
                        bbuf.at[k, part[p]],
                        (to_x, to_y)[p],
                    )
    for k in (2, 1, 3, 0):
        for p in range(2):
            arrived(32 + k * 2 + p, bbuf.at[k, part[p]])
            bbuf[k, part[p]] = bbuf[k, part[p]] + abuf[k * 2, part[p]]
            if k:
                push(
                    40 + (k - 1) * 2 + p,
                    bbuf.at[k, part[p]],
                    zbuf.at[k - 1, part[p]],
                    to_z[k],
                )
    out[...] = bbuf[0].astype(F32)
    for k in (1, 3, 2):
        for p in range(2):
            arrived(40 + (k - 1) * 2 + p, zbuf.at[k - 1, part[p]])
            out[part[p]] = out[part[p]] + zbuf[k - 1, part[p]].astype(F32)
    for one in started:
        one.wait_send()


def reduce_call(terms):
    shape = terms.shape[1:]
    cut = shape[0] // 32 * 16
    return pl.pallas_call(
        functools.partial(reduce_kernel, cut),
        out_shape=jax.ShapeDtypeStruct(shape, F32),
        in_specs=[pl.BlockSpec(memory_space=pl.ANY)],
        out_specs=pl.BlockSpec(memory_space=pltpu.VMEM),
        scratch_shapes=[
            pltpu.VMEM((16,) + shape, BF),
            pltpu.VMEM((16,) + shape, BF),
            pltpu.VMEM((8,) + shape, BF),
            pltpu.VMEM((4,) + shape, BF),
            pltpu.VMEM((3,) + shape, BF),
            pltpu.SemaphoreType.DMA((46,)),
            pltpu.SemaphoreType.DMA((46,)),
            pltpu.SemaphoreType.DMA((16,)),
        ],
        compiler_params=pltpu.CompilerParams(
            collective_id=1, has_side_effects=True, vmem_limit_bytes=26 * 1024 * 1024
        ),
        name="reduce_gradients",
    )(terms)


def exchange_kernel(g_ref, out, buf, send, recv):
    z, x, y, c = coordinates()
    others = ((y, 1 - c), (1 - y, c), (1 - y, 1 - c))
    greet([device(z, x, *other) for other in others])
    started = []
    for i in (2, 1, 0):
        yy, cc = others[i]
        one = pltpu.make_async_remote_copy(
            src_ref=g_ref.at[yy * 2 + cc],
            dst_ref=buf.at[i],
            send_sem=send.at[i],
            recv_sem=recv.at[i],
            device_id=device(z, x, yy, cc),
            device_id_type=MESH,
        )
        one.start()
        started.append(one)
    out[...] = g_ref[y * 2 + c].astype(F32)
    for one, i in zip(started[::-1], range(3)):
        one.wait_recv()
        out[...] = out[...] + buf[i].astype(F32)
    for one in started:
        one.wait_send()


def exchange_call(terms):
    shape = terms.shape[1:]
    return pl.pallas_call(
        exchange_kernel,
        out_shape=jax.ShapeDtypeStruct(shape, F32),
        in_specs=[pl.BlockSpec(memory_space=pltpu.VMEM)],
        out_specs=pl.BlockSpec(memory_space=pltpu.VMEM),
        scratch_shapes=[
            pltpu.VMEM((3,) + shape, BF),
            pltpu.SemaphoreType.DMA((3,)),
            pltpu.SemaphoreType.DMA((3,)),
        ],
        compiler_params=pltpu.CompilerParams(
            collective_id=2, has_side_effects=True, vmem_limit_bytes=16 * 1024 * 1024
        ),
        name="exchange_keys",
    )(terms)


def body(
    kernels, tokens, cotangent, segments, gains, w_query, w_key, w_value, w_out, w_gate, w_up, w_down
):
    resid = tokens[0].astype(F32)
    rows = resid.shape[0]
    cycle = lax.axis_size("ctx")
    groups = lax.axis_size("dp")
    devices = cycle * groups
    place = lax.axis_index("ctx")
    scale = HD ** (-0.5)
    doc_local = segments[0]
    own = (w_query.T, w_key.T, w_value.T, w_out, w_gate.T, w_up.T, w_down)
    own += (jnp.pad(gains[None], ((0, 0), (0, D - gains.shape[0]))),)
    counts = [piece.shape[0] for piece in own]
    starts = [sum(counts[:i]) for i in range(len(counts))]
    height = -(-sum(counts) // 16) * 16 if kernels else sum(counts)
    packed = jnp.pad(jnp.concatenate(own, axis=0), ((0, height - sum(counts)), (0, 0)))
    if kernels:
        marks = jnp.pad(doc_local.astype(BF)[None], ((0, 15), (0, D - rows)))
        every, near = gather_call(
            packed, jnp.concatenate([tokens[0], marks], axis=0), devices, cycle
        )
        tokens_all = near[:, :rows].reshape(cycle * rows, D)
        doc_all = near[:, rows, :rows].reshape(cycle * rows).astype(jnp.int32)
    else:
        every = lax.all_gather(packed, ("dp", "ctx"), axis=0, tiled=False)
        tokens_all = lax.all_gather(tokens[0], "ctx", axis=0, tiled=True)
        doc_all = lax.all_gather(doc_local, "ctx", axis=0, tiled=True)
    wq, wk, wv, wo, wg, wu, wd = [
        every[:, s : s + n].reshape(devices * n, D) for s, n in zip(starts[:7], counts[:7])
    ]
    gain_all = every[:, starts[7], : gains.shape[0]].reshape(-1).astype(F32)
    g_in = gain_all[0:D]
    g_post_attn = gain_all[D : 2 * D]
    g_pre_ff = gain_all[2 * D : 3 * D]
    g_post_ff = gain_all[3 * D : 4 * D]
    g_query = gain_all[4 * D : 4 * D + HD]
    g_key = gain_all[4 * D + HD : 4 * D + 2 * HD]

    normed_f, in_factor = norm_forward(resid, g_in)
    normed = normed_f.astype(BF)
    normed_all = norm_forward(tokens_all.astype(F32), g_in)[0].astype(BF)
    queries = against(normed, wq).reshape(rows, H, HD)
    keys_all = against(normed_all, wk)
    values_all = against(normed_all, wv).astype(BF)
    positions = place * rows + jnp.arange(rows, dtype=jnp.int32)
    cos_all, sin_all = rotary_tables(jnp.arange(cycle * rows, dtype=jnp.int32), HD)
    cosine = lax.dynamic_slice_in_dim(cos_all, place * rows, rows, 0)
    sine = lax.dynamic_slice_in_dim(sin_all, place * rows, rows, 0)
    query_normed, query_factor = norm_forward(queries, g_query)
    key_normed, key_factor_all = norm_forward(keys_all, g_key)
    keys = lax.dynamic_slice_in_dim(keys_all, place * rows, rows, 0)
    key_factor = lax.dynamic_slice_in_dim(key_factor_all, place * rows, rows, 0)
    query_rot = (rotate(query_normed, cosine[:, None, :], sine[:, None, :]) * scale).astype(BF)
    key_rot = rotate(key_normed, cos_all, sin_all).astype(BF)
    query_rows = jnp.transpose(query_rot, (1, 0, 2)).reshape(H * rows, HD)
    query_pos = jnp.tile(positions, H)
    query_doc = jnp.tile(doc_local, H)
    key_pos = jnp.arange(cycle * rows, dtype=jnp.int32)
    allowed = (key_pos[None, :] <= query_pos[:, None]) & (doc_all[None, :] == query_doc[:, None])
    masked = jnp.where(allowed, against(query_rows, key_rot), NEGATIVE)
    top = jnp.max(masked, axis=1, keepdims=True)
    weights = jnp.where(allowed, jnp.exp(masked - top), 0.0)
    probs = weights / jnp.sum(weights, axis=1, keepdims=True)
    probs_low = probs.astype(BF)
    probs_rest = (probs - probs_low.astype(F32)).astype(BF)
    attended_rows = product(probs_low, values_all) + product(probs_rest, values_all)
    attended = jnp.transpose(attended_rows.reshape(H, rows, HD), (1, 0, 2))
    heads = attended.reshape(rows, H * HD).astype(BF)
    branch = product(heads, wo)
    attn_normed, branch_factor = norm_forward(branch, g_post_attn)
    hidden = resid + attn_normed
    ff_f, ff_factor = norm_forward(hidden, g_pre_ff)
    ff_in = ff_f.astype(BF)
    gate = against(ff_in, wg)
    up_proj = against(ff_in, wu)
    mid = gelu_mix(gate, up_proj).astype(BF)
    down = product(mid, wd)
    down_normed, down_factor = norm_forward(down, g_post_ff)
    mixed = (hidden + down_normed).astype(BF)

    grad_out = cotangent[0].astype(F32)
    grad_down_f, grad_g_post_ff = norm_backward(down, down_factor, g_post_ff, grad_out)
    grad_down = grad_down_f.astype(BF)
    w_down_part = inner_rows(mid, grad_down)
    grad_mid = against(grad_down, wd)
    _, gelu_back = jax.vjp(gelu_mix, gate, up_proj)
    grad_gate_f, grad_up_f = gelu_back(grad_mid)
    grad_gate = grad_gate_f.astype(BF)
    grad_up = grad_up_f.astype(BF)
    w_gate_part = inner_rows(grad_gate, ff_in)
    w_up_part = inner_rows(grad_up, ff_in)
    grad_ff = product(grad_gate, wg) + product(grad_up, wu)
    hidden_part, grad_g_pre_ff = norm_backward(hidden, ff_factor, g_pre_ff, grad_ff)
    grad_hidden = grad_out + hidden_part
    grad_branch_f, grad_g_post_attn = norm_backward(branch, branch_factor, g_post_attn, grad_hidden)
    grad_branch = grad_branch_f.astype(BF)
    w_out_part = inner_rows(heads, grad_branch)
    grad_att = against(grad_branch, wo).reshape(rows, H, HD).astype(BF)
    grad_rows = jnp.transpose(grad_att, (1, 0, 2)).reshape(H * rows, HD)
    delta = jnp.sum(grad_rows.astype(F32) * attended_rows, axis=1, keepdims=True)
    grad_probs = against(grad_rows, values_all)
    grad_logits = (probs * (grad_probs - delta)).astype(BF)
    grad_qrows = product(grad_logits, key_rot)
    grad_key_part = inner_rows(grad_logits, query_rows)
    grad_value_part = inner_rows(probs_low, grad_rows)
    grad_kv = jnp.concatenate([grad_key_part, grad_value_part], axis=1)
    if kernels:
        key_grad = exchange_call(grad_kv.astype(BF).reshape(cycle, rows, 2 * HD))
    else:
        key_grad = lax.psum_scatter(grad_kv, "ctx", scatter_dimension=0, tiled=True)
    grad_krot = key_grad[:, :HD]
    grad_values = key_grad[:, HD:].astype(BF)
    grad_qrot = jnp.transpose(grad_qrows.reshape(H, rows, HD), (1, 0, 2))
    grad_qn = rotate(grad_qrot * scale, cosine[:, None, :], -sine[:, None, :])
    grad_queries_f, grad_g_query = norm_backward(queries, query_factor, g_query, grad_qn)
    grad_queries = grad_queries_f.reshape(rows, H * HD).astype(BF)
    grad_kn = rotate(grad_krot, cosine, -sine)
    grad_keys_f, grad_g_key = norm_backward(keys, key_factor, g_key, grad_kn)
    grad_keys = grad_keys_f.astype(BF)
    w_query_part = inner_rows(grad_queries, normed)
    w_key_part = inner_rows(grad_keys, normed)
    w_value_part = inner_rows(grad_values, normed)
    grad_normed = product(grad_queries, wq) + product(grad_keys, wk) + product(grad_values, wv)
    input_part, grad_g_in = norm_backward(resid, in_factor, g_in, grad_normed)
    tokens_grad = (grad_hidden + input_part).astype(BF)
    gains_part = jnp.concatenate(
        [grad_g_in, grad_g_post_attn, grad_g_pre_ff, grad_g_post_ff, grad_g_query, grad_g_key]
    ).reshape(devices, 1, -1)
    terms = [
        part.reshape(devices, -1, D)
        for part in (
            w_query_part,
            w_key_part,
            w_value_part,
            w_out_part,
            w_gate_part,
            w_up_part,
            w_down_part,
        )
    ]
    tail = ((0, 0), (0, height - sum(counts)), (0, D - gains.shape[0]))
    terms.append(jnp.pad(gains_part, tail))
    kind = BF if kernels else F32
    stacked = jnp.concatenate([term.astype(kind) for term in terms], axis=1)
    if kernels:
        owned = reduce_call(stacked)
    else:
        owned = lax.psum_scatter(stacked, ("dp", "ctx"), scatter_dimension=0, tiled=False)
    q, k, v, o, g, u, d, s = [owned[a : a + n] for a, n in zip(starts, counts)]
    return (
        mixed[None],
        tokens_grad[None],
        s[0, : gains.shape[0]],
        q.T,
        k.T,
        v.T,
        o,
        g.T,
        u.T,
        d,
    )


def solution(mesh):
    kernels = (mesh.shape["dp"], mesh.shape["ctx"]) == (8, 4)
    return jax.shard_map(
        functools.partial(body, kernels),
        mesh=mesh,
        in_specs=(
            P("dp", "ctx", None),
            P("dp", "ctx", None),
            P("dp", "ctx"),
            P(("dp", "ctx")),
            P(None, ("dp", "ctx")),
            P(None, ("dp", "ctx")),
            P(None, ("dp", "ctx")),
            P(("dp", "ctx"), None),
            P(None, ("dp", "ctx")),
            P(None, ("dp", "ctx")),
            P(("dp", "ctx"), None),
        ),
        out_specs=(
            P("dp", "ctx", None),
            P("dp", "ctx", None),
            P(("dp", "ctx")),
            P(None, ("dp", "ctx")),
            P(None, ("dp", "ctx")),
            P(None, ("dp", "ctx")),
            P(("dp", "ctx"), None),
            P(None, ("dp", "ctx")),
            P(None, ("dp", "ctx")),
            P(("dp", "ctx"), None),
        ),
        check_vma=False,
    )
```
